512 devices in a mesh: cin: 16 (over z), cout: 8 (over y, core), sp: 4 (over x).
Axes of the slice: x: 4, y: 4, z: 16, core: 2. Of those that a mesh axis runs over, the one named last changes fastest.
Arguments:
- activations: bfloat16 [512, 4, 32, 128], P('cin', 'sp', 'cout'), may hold values from -6 to 6
- weights: bfloat16 [3, 3, 3, 512, 512], P(None, None, None, 'cin', 'cout'), may hold values from -0.0546875 to 0.0546875
- out_grad: bfloat16 [512, 4, 32, 128], P('cout', 'sp', 'cin'), may hold values from -6 to 6
Outputs:
- output: bfloat16 [512, 4, 32, 128], P('cout', 'sp', 'cin')
- in_grad: bfloat16 [512, 4, 32, 128], P('cin', 'sp', 'cout')
- weight_grad: bfloat16 [3, 3, 3, 512, 512], P(None, None, None, 'cin', 'cout')
The draws below stay inside these ranges and needn't reach their ends.
All inputs are finite; a program needn't handle non-finite values.
Results may differ from the reference program's by a relative error of at most 0.001.
Values may be sent and summed in bfloat16 or wider, within the bound.
No kernel may reach another device: no remote copies, remote signals or barrier semaphores. Data moves between devices by JAX's collectives and lax.ppermute only.
A program may use at most 64 MiB of HBM per device.

```python
import math
import jax
import jax.numpy as jnp
from jax import lax

CIN = 512
COUT = 512
H = 32
W = 128
DEPTH = 4
VOXELS = 16384


def spiked(values, rng, source, target, parts, factor):
    def block_of(axis_at):
        return (jnp.arange(values.shape[axis_at]) // (values.shape[axis_at] // parts)).reshape((-1,) + (1,) * (values.ndim - 1 - axis_at))

    first = jax.random.permutation(rng, parts)[block_of(target)]
    far = (block_of(target) + parts // 2) % parts
    return jnp.where((block_of(source) == first) | (block_of(source) == far), factor * values, values)


def block_scale(rng, extent, pieces, low, high):
    loudness, own = 1.0, jax.random.fold_in(rng, 6)
    for position, parts in pieces:
        steps = jnp.exp(jax.random.uniform(jax.random.fold_in(own, position), (parts,), jnp.float32, low / len(pieces), high / len(pieces)))
        loudness = loudness * jnp.repeat(steps, extent[position] // parts).reshape([-1 if axis == position else 1 for axis in range(len(extent))])
    return loudness


def normal_values(stream_key, extent, deviation, limit, cuts=(), held_as=jnp.bfloat16):
    values = jax.random.normal(stream_key, extent, jnp.float32) * deviation
    if len(cuts) > 0:
        values = block_scale(stream_key, extent, cuts, -0.22, 0.18) * values
    return jnp.clip(values, min=-limit, max=limit).astype(held_as)


def heavy_noise(own_key, shape, scale, reach, pieces, heavy, kind=jnp.bfloat16):
    array = scale * jax.random.normal(own_key, shape, jnp.float32)
    if pieces:
        array = array * block_scale(own_key, shape, pieces, -0.22, 0.18)
    return jnp.clip(spiked(array, jax.random.fold_in(own_key, 3), *heavy), -reach, reach).astype(kind)


def setup_inputs(seed: int = 0) -> dict:
    keys = jax.random.split(jax.random.key(seed), 4)
    activations = heavy_noise(keys[0], (CIN, DEPTH, H, W), 1.0, 6.0, ((0, 16), (1, 4), (2, 8)), (0, 2, 16, 2.0))
    weights = normal_values(keys[1], (3, 3, 3, CIN, COUT), (27 * CIN) ** -0.5, 0.0546875, ((3, 16), (4, 8)))
    out_grad = heavy_noise(keys[2], (COUT, DEPTH, H, W), 1.0, 6.0, ((0, 8), (1, 4), (2, 16)), (0, 2, 16, 2.0))
    return {"activations": activations, "weights": weights, "out_grad": out_grad}


def conv_same(field, kernel):
    return lax.conv_general_dilated(field[None], kernel, (1, 1, 1), [(1, 1), (1, 1), (1, 1)], dimension_numbers=('NCDHW', 'DHWIO', 'NCDHW'), precision=lax.Precision.HIGHEST)[0]

def reference(activations, weights, out_grad):
    x_float = activations.astype(jnp.float32)
    w_float = weights.astype(jnp.float32)
    g_float = out_grad.astype(jnp.float32)
    output = conv_same(x_float, w_float).astype(jnp.bfloat16)
    flipped = jnp.transpose(w_float[::-1, ::-1, ::-1], (0, 1, 2, 4, 3))
    in_grad = conv_same(g_float, flipped).astype(jnp.bfloat16)
    padded = jnp.pad(x_float, ((0, 0), (1, 1), (1, 1), (1, 1)))
    tap_terms = []
    for a in range(3):
        for b in range(3):
            for c in range(3):
                window = padded[:, a:a + DEPTH, b:b + H, c:c + W]
                tap_terms.append(jnp.einsum('cdhw,odhw->co', window, g_float, precision=lax.Precision.HIGHEST))
    summed = jnp.stack(tap_terms).reshape(3, 3, 3, CIN, COUT)
    weight_grad = (summed * (1.0 / math.sqrt(VOXELS))).astype(jnp.bfloat16)
    return (output, in_grad, weight_grad)
```

```python
import math

import jax
import jax.numpy as jnp
from jax import lax
from jax.experimental import pallas as pl
from jax.experimental.pallas import tpu as pltpu
from jax.sharding import PartitionSpec as P

F32 = jnp.float32
BF16 = jnp.bfloat16
VMEM_LIMIT = 40 * 1024 * 1024


def shifted(plane, step):
    if step == 0:
        return plane
    width = plane.shape[-1]
    moved = pltpu.roll(plane.astype(F32), (-step) % width, plane.ndim - 1)
    lane = lax.broadcasted_iota(jnp.int32, plane.shape, plane.ndim - 1)
    edge = width - 1 if step > 0 else 0
    return jnp.where(lane == edge, 0.0, moved).astype(plane.dtype)


def stack_taps(planes, stacked):
    rows, channels, width = planes[0].shape
    for a, plane in enumerate(planes):
        value = plane[...]
        for c in range(3):
            moved = shifted(value, c - 1)
            at = (a * 3 + c) * channels
            for h in range(rows):
                stacked[at : at + channels, h * width : (h + 1) * width] = moved[h]


def add_row_taps(product, out, channels, rows, width):
    for h in range(rows):
        total = None
        for b in range(3):
            row = h + b - 1
            if 0 <= row < rows:
                part = product[b * channels : (b + 1) * channels, row * width : (row + 1) * width]
                total = part if total is None else total + part
        out[h] = total


def forward_kernel(low, mid, high, weights, out, stacked, product):
    rows, cin, width = mid.shape
    cout = weights.shape[-1]
    stack_taps((low, mid, high), stacked)
    blocks = [
        jnp.concatenate([weights[a, b, c] for a in range(3) for c in range(3)], axis=0)
        for b in range(3)
    ]
    kernel = jnp.concatenate([jnp.transpose(block.astype(F32)) for block in blocks], axis=0)
    product[...] = jnp.dot(kernel.astype(BF16), stacked[...], preferred_element_type=F32)
    add_row_taps(product, out, cout, rows, width)


def backward_kernel(low, mid, high, weights, out, stacked, product):
    rows, cout, width = mid.shape
    cin = weights.shape[-2]
    stack_taps((low, mid, high), stacked)
    kernel = jnp.concatenate(
        [
            jnp.concatenate(
                [weights[2 - a, 2 - b, 2 - c] for a in range(3) for c in range(3)], axis=1
            )
            for b in range(3)
        ],
        axis=0,
    )
    product[...] = jnp.dot(kernel, stacked[...], preferred_element_type=F32)
    add_row_taps(product, out, cin, rows, width)


def kernel_grad_kernel(low, mid, high, grad, out, stacked, shifted_grad):
    rows, cin, width = mid.shape
    cout = grad.shape[1]
    stack_taps((low, mid, high), stacked)
    for b in range(3):
        for h in range(rows):
            row = h - (b - 1)
            value = grad[row] if 0 <= row < rows else jnp.zeros((cout, width), BF16)
            shifted_grad[b * cout : (b + 1) * cout, h * width : (h + 1) * width] = value
    taps = lax.dot_general(
        stacked[...], shifted_grad[...], (((1,), (1,)), ((), ())), preferred_element_type=F32
    )
    half = taps.shape[0] // 2
    first = taps[:, : 2 * cout]
    second = jnp.concatenate([taps[:half, 2 * cout :], taps[half:, 2 * cout :]], axis=1)
    rest = out.shape[0] - first.shape[0] - half
    out[: 2 * half] = first
    out[2 * half : 3 * half] = second
    out[3 * half :] = jnp.zeros((rest, 2 * cout), F32)


def kernel_grad_finish(parts, out, scale):
    total = (parts[0] + parts[1]) + (parts[2] + parts[3])
    taps = (total * scale).astype(BF16)
    cin, cout = out.shape[-2:]
    half = 9 * cin // 2
    for a in range(3):
        for c in range(3):
            at = (a * 3 + c) * cin
            for b in range(2):
                out[a, b, c] = taps[at : at + cin, b * cout : (b + 1) * cout]
            for lo in range(at, at + cin, cin // 2):
                side = lo // half
                row = 2 * half + lo - side * half
                out[a, 2, c, lo - at : lo - at + cin // 2] = taps[
                    row : row + cin // 2, side * cout : (side + 1) * cout
                ]


def call(kernel, out, scratch, flops, *args):
    moved = sum(math.prod(a.shape) * a.dtype.itemsize for a in args)
    return pl.pallas_call(
        kernel,
        out_shape=out,
        scratch_shapes=scratch,
        compiler_params=pltpu.CompilerParams(vmem_limit_bytes=VMEM_LIMIT),
        cost_estimate=pl.CostEstimate(flops=flops, bytes_accessed=moved, transcendentals=0),
    )(*args)


def halos(plane, axis):
    count = lax.axis_size(axis)
    forward = [(i, i + 1) for i in range(count - 1)]
    backward = [(i + 1, i) for i in range(count - 1)]
    return lax.ppermute(plane, axis, forward), lax.ppermute(plane, axis, backward)


def body(activations, weights, out_grad):
    cin, cout = weights.shape[3:]
    width = activations.shape[-1]
    x_own = jnp.transpose(activations[:, 0], (1, 0, 2))
    g_own = jnp.transpose(out_grad[:, 0], (1, 0, 2))
    x_mid = lax.all_gather(x_own, "cout", axis=0, tiled=True)
    rows = x_mid.shape[0]
    voxels = rows * width
    flops = 2 * 27 * cin * cout * voxels
    x_low, x_high = halos(x_mid, "sp")

    partial_out = call(
        forward_kernel,
        jax.ShapeDtypeStruct((rows, cout, width), F32),
        [pltpu.VMEM((9 * cin, voxels), BF16), pltpu.VMEM((3 * cout, voxels), F32)],
        flops,
        x_low,
        x_mid,
        x_high,
        weights,
    )
    out_parts = lax.all_to_all(partial_out, "cin", 0, 0, tiled=True)

    g_mid = lax.all_gather(g_own, "cin", axis=0, tiled=True)
    g_low, g_high = halos(g_mid, "sp")
    packed_rows = -(-27 * cin // 2 // 32) * 32
    local_grad = call(
        kernel_grad_kernel,
        jax.ShapeDtypeStruct((packed_rows, 2 * cout), F32),
        [pltpu.VMEM((9 * cin, voxels), BF16), pltpu.VMEM((3 * cout, voxels), BF16)],
        flops,
        x_low,
        x_mid,
        x_high,
        g_mid,
    )
    depth = lax.axis_size("sp")
    grad_parts = lax.all_to_all(
        jnp.broadcast_to(local_grad, (depth,) + local_grad.shape), "sp", 0, 0, tiled=True
    )
    partial_dx = call(
        backward_kernel,
        jax.ShapeDtypeStruct((rows, cin, width), F32),
        [pltpu.VMEM((9 * cout, voxels), BF16), pltpu.VMEM((3 * cin, voxels), F32)],
        flops,
        g_low,
        g_mid,
        g_high,
        weights,
    )
    dx_parts = lax.all_to_all(partial_dx, "cout", 0, 0, tiled=True)

    scale = 1.0 / math.sqrt(depth * voxels)
    weight_grad = call(
        lambda parts, out: kernel_grad_finish(parts, out, scale),
        jax.ShapeDtypeStruct(weights.shape, BF16),
        [],
        27 * cin * cout * depth,
        grad_parts,
    )

    def total(parts, like, axis):
        summed = jnp.sum(parts.reshape((lax.axis_size(axis), -1) + parts.shape[1:]), axis=0)
        return jnp.transpose(summed, (1, 0, 2)).astype(BF16).reshape(like.shape)

    in_grad = total(dx_parts, activations, "cout")
    output = total(out_parts, out_grad, "cin")
    return output, in_grad, weight_grad


def solution(mesh):
    placed = (
        P("cin", "sp", "cout", None),
        P(None, None, None, "cin", "cout"),
        P("cout", "sp", "cin", None),
    )
    return jax.shard_map(
        body,
        mesh=mesh,
        in_specs=placed,
        out_specs=(
            P("cout", "sp", "cin", None),
            P("cin", "sp", "cout", None),
            P(None, None, None, "cin", "cout"),
        ),
        check_vma=False,
    )
```

```python
import functools
import math

import jax
import jax.numpy as jnp
from jax import lax
from jax.experimental import pallas as pl
from jax.experimental.pallas import tpu as pltpu
from jax.sharding import PartitionSpec as P

F32 = jnp.float32
BF16 = jnp.bfloat16
VMEM_LIMIT = 40 * 1024 * 1024


def shifted(plane, step):
    if step == 0:
        return plane
    width = plane.shape[-1]
    moved = pltpu.roll(plane.astype(F32), (-step) % width, plane.ndim - 1)
    lane = lax.broadcasted_iota(jnp.int32, plane.shape, plane.ndim - 1)
    edge = width - 1 if step > 0 else 0
    return jnp.where(lane == edge, 0.0, moved).astype(plane.dtype)


def stack_taps(planes, stacked):
    rows, channels, width = planes[0].shape
    for a, plane in enumerate(planes):
        value = plane[...]
        for c in range(3):
            moved = shifted(value, c - 1)
            at = (a * 3 + c) * channels
            for h in range(rows):
                stacked[at : at + channels, h * width : (h + 1) * width] = moved[h]


def add_row_taps(product, out, channels, rows, width):
    for h in range(rows):
        total = None
        for b in range(3):
            row = h + b - 1
            if 0 <= row < rows:
                part = product[b * channels : (b + 1) * channels, row * width : (row + 1) * width]
                total = part if total is None else total + part
        out[h] = total


def forward_kernel(place, low, mid, high, weights, own, ahead, behind, far_a, far_b, stacked, product):
    rows, cin, width = mid.shape
    cout = weights.shape[-1]
    stack_taps((low, mid, high), stacked)
    blocks = [
        jnp.concatenate([weights[a, b, c] for a in range(3) for c in range(3)], axis=0)
        for b in range(3)
    ]
    kernel = jnp.concatenate([jnp.transpose(block.astype(F32)) for block in blocks], axis=0)
    product[:, width:-width] = jnp.dot(
        kernel.astype(BF16), stacked[...], preferred_element_type=F32
    )
    edge = jnp.zeros((product.shape[0], width), F32)
    product[:, :width] = edge
    product[:, -width:] = edge
    repeats, each = own.shape[:2]
    ways = rows // (repeats * each)
    for slot in range(ways):
        kind = lax.rem(place[0] + slot, ways)
        for q in range(repeats):
            for e in range(each):
                row = (q * ways + kind) * each + e
                total = None
                for b in range(3):
                    at = pl.multiple_of((row + b) * width, width)
                    part = product[b * cout : (b + 1) * cout, pl.ds(at, width)]
                    total = part if total is None else total + part
                if slot == 0:
                    own[q, e] = total
                elif slot == 1:
                    ahead[q, e] = total
                elif slot == 2:
                    far_a[q, e] = total[: cout // 2]
                    far_b[q, e] = total[cout // 2 :]
                else:
                    behind[q, e] = total


def near_sum_kernel(own, ahead, behind, far_a, far_b, out):
    half = far_a.shape[2]
    near = own[...] + (ahead[...] + behind[...])
    out[:, :, :half] = near[:, :, :half] + far_a[...]
    out[:, :, half:] = near[:, :, half:] + far_b[...]


def backward_kernel(low, mid, high, weights, out, stacked, product):
    rows, cout, width = mid.shape
    cin = weights.shape[-2]
    stack_taps((low, mid, high), stacked)
    kernel = jnp.concatenate(
        [
            jnp.concatenate(
                [weights[2 - a, 2 - b, 2 - c] for a in range(3) for c in range(3)], axis=1
            )
            for b in range(3)
        ],
        axis=0,
    )
    product[...] = jnp.dot(kernel, stacked[...], preferred_element_type=F32)
    add_row_taps(product, out, cin, rows, width)


def kernel_grad_kernel(low, mid, high, grad, out, stacked, shifted_grad):
    rows, cin, width = mid.shape
    cout = grad.shape[1]
    stack_taps((low, mid, high), stacked)
    for b in range(3):
        for h in range(rows):
            row = h - (b - 1)
            value = grad[row] if 0 <= row < rows else jnp.zeros((cout, width), BF16)
            shifted_grad[b * cout : (b + 1) * cout, h * width : (h + 1) * width] = value
    taps = lax.dot_general(
        stacked[...], shifted_grad[...], (((1,), (1,)), ((), ())), preferred_element_type=F32
    )
    half = taps.shape[0] // 2
    first = taps[:, : 2 * cout]
    second = jnp.concatenate([taps[:half, 2 * cout :], taps[half:, 2 * cout :]], axis=1)
    rest = out.shape[0] - first.shape[0] - half
    out[: 2 * half] = first
    out[2 * half : 3 * half] = second
    out[3 * half :] = jnp.zeros((rest, 2 * cout), F32)


def kernel_grad_finish(scale, near, far, out):
    taps = ((near[...] + far[...]) * scale).astype(BF16)
    cin, cout = out.shape[-2:]
    half = 9 * cin // 2
    for a in range(3):
        for c in range(3):
            at = (a * 3 + c) * cin
            for b in range(2):
                out[a, b, c] = taps[at : at + cin, b * cout : (b + 1) * cout]
            for lo in range(at, at + cin, cin // 2):
                side = lo // half
                row = 2 * half + lo - side * half
                out[a, 2, c, lo - at : lo - at + cin // 2] = taps[
                    row : row + cin // 2, side * cout : (side + 1) * cout
                ]


def call(kernel, out, scratch, flops, *args):
    moved = sum(math.prod(a.shape) * a.dtype.itemsize for a in args)
    specs = [pl.BlockSpec(memory_space=pltpu.SMEM if a.ndim == 1 else pltpu.VMEM) for a in args]
    return pl.pallas_call(
        kernel,
        out_shape=out,
        in_specs=specs,
        scratch_shapes=scratch,
        compiler_params=pltpu.CompilerParams(vmem_limit_bytes=VMEM_LIMIT),
        cost_estimate=pl.CostEstimate(flops=flops, bytes_accessed=moved, transcendentals=0),
    )(*args)


def halos(plane, axis):
    count = lax.axis_size(axis)
    forward = [(i, i + 1) for i in range(count - 1)]
    backward = [(i + 1, i) for i in range(count - 1)]
    return lax.ppermute(plane, axis, forward), lax.ppermute(plane, axis, backward)


def around(block, axis, step):
    count = lax.axis_size(axis)
    return lax.ppermute(block, axis, [(i, (i + step) % count) for i in range(count)])


def exchange(blocks, axis, groups=None):
    return lax.all_to_all(blocks, axis, 0, 0, tiled=True, axis_index_groups=groups)


def gather(block, axis, count, groups=None):
    copies = jnp.broadcast_to(block[None], (count,) + block.shape)
    return exchange(copies, axis, groups).reshape((-1,) + block.shape[1:])


def body(activations, weights, out_grad):
    cin, cout = weights.shape[3:]
    width = activations.shape[-1]
    ring = lax.axis_size("cin")
    depth = lax.axis_size("sp")
    ways = 4
    repeats = ring // ways
    apart = [[ways * q + r for q in range(repeats)] for r in range(ways)]
    x_own = jnp.transpose(activations[:, 0], (1, 0, 2))
    g_own = jnp.transpose(out_grad[:, 0], (1, 0, 2))
    each = g_own.shape[0]

    g_mid = gather(g_own, "cin", ring)
    x_mid = lax.all_gather(x_own, "cout", axis=0, tiled=True)
    rows = x_mid.shape[0]
    voxels = rows * width
    flops = 2 * 27 * cin * cout * voxels
    x_low, x_high = halos(x_mid, "sp")

    piece = jax.ShapeDtypeStruct((repeats, each, cout, width), F32)
    half_piece = jax.ShapeDtypeStruct((repeats, each, cout // 2, width), F32)
    place = lax.axis_index("cin").astype(jnp.int32).reshape(1)
    own, ahead, behind, far_a, far_b = call(
        forward_kernel,
        (piece, piece, piece, half_piece, half_piece),
        [
            pltpu.VMEM((9 * cin, voxels), BF16),
            pltpu.VMEM((3 * cout, voxels + 2 * width), F32),
        ],
        flops,
        place,
        x_low,
        x_mid,
        x_high,
        weights,
    )
    near_sum = call(
        near_sum_kernel,
        piece,
        [],
        4 * math.prod(piece.shape),
        own,
        around(ahead, "cin", 1),
        around(behind, "cin", -1),
        around(far_a, "cin", 2),
        around(far_b, "cin", -2),
    )
    out_parts = exchange(near_sum, "cin", apart)

    g_low, g_high = halos(g_mid, "sp")
    packed_rows = -(-27 * cin // 2 // 32) * 32
    local_grad = call(
        kernel_grad_kernel,
        jax.ShapeDtypeStruct((packed_rows, 2 * cout), F32),
        [pltpu.VMEM((9 * cin, voxels), BF16), pltpu.VMEM((3 * cout, voxels), BF16)],
        flops,
        x_low,
        x_mid,
        x_high,
        g_mid,
    )
    pair_grad = local_grad + lax.ppermute(local_grad, "sp", [(i, i ^ 1) for i in range(depth)])
    far_grad = lax.ppermute(pair_grad, "sp", [(i, depth - 1 - i) for i in range(depth)])
    partial_dx = call(
        backward_kernel,
        jax.ShapeDtypeStruct((rows, cin, width), F32),
        [pltpu.VMEM((9 * cout, voxels), BF16), pltpu.VMEM((3 * cin, voxels), F32)],
        flops,
        g_low,
        g_mid,
        g_high,
        weights,
    )
    dx_parts = exchange(partial_dx, "cout")

    scale = 1.0 / math.sqrt(depth * voxels)
    weight_grad = call(
        functools.partial(kernel_grad_finish, scale),
        jax.ShapeDtypeStruct(weights.shape, BF16),
        [],
        27 * cin * cout * 2,
        pair_grad,
        far_grad,
    )

    def total(parts, like):
        parts = parts.reshape((-1, like.shape[2]) + parts.shape[-2:])
        summed = jnp.sum(parts, axis=0)
        return jnp.transpose(summed, (1, 0, 2)).astype(BF16).reshape(like.shape)

    return total(out_parts, out_grad), total(dx_parts, activations), weight_grad


def solution(mesh):
    placed = (
        P("cin", "sp", "cout", None),
        P(None, None, None, "cin", "cout"),
        P("cout", "sp", "cin", None),
    )
    return jax.shard_map(
        body,
        mesh=mesh,
        in_specs=placed,
        out_specs=(
            P("cout", "sp", "cin", None),
            P("cin", "sp", "cout", None),
            P(None, None, None, "cin", "cout"),
        ),
        check_vma=False,
    )
```

```python
import functools
import math

import jax
import jax.numpy as jnp
from jax import lax
from jax.experimental import pallas as pl
from jax.experimental.pallas import tpu as pltpu
from jax.sharding import PartitionSpec as P

F32 = jnp.float32
BF16 = jnp.bfloat16
VMEM_LIMIT = 40 * 1024 * 1024


def shifted(plane, step):
    if step == 0:
        return plane
    width = plane.shape[-1]
    moved = pltpu.roll(plane.astype(F32), (-step) % width, plane.ndim - 1)
    lane = lax.broadcasted_iota(jnp.int32, plane.shape, plane.ndim - 1)
    edge = width - 1 if step > 0 else 0
    return jnp.where(lane == edge, 0.0, moved).astype(plane.dtype)


def stack_taps(planes, stacked):
    rows, channels, width = planes[0].shape
    for a, plane in enumerate(planes):
        value = plane
        for c in range(3):
            moved = shifted(value, c - 1)
            at = (a * 3 + c) * channels
            for h in range(rows):
                stacked[at : at + channels, h * width : (h + 1) * width] = moved[h]


def row_total(product, channels, row, width):
    total = None
    for b in range(3):
        at = pl.multiple_of((row + b) * width, width)
        part = product[b * channels : (b + 1) * channels, pl.ds(at, width)]
        total = part if total is None else total + part
    return total


def forward_kernel(place, planes, weights, own, ahead, far, behind, stacked, product):
    cin, width = planes.shape[-2:]
    rows = planes.shape[0] * planes.shape[2]
    cout = weights.shape[-1]
    stack_taps([planes[:, a].reshape(rows, cin, width) for a in range(3)], stacked)
    blocks = [
        jnp.concatenate([weights[a, b, c] for a in range(3) for c in range(3)], axis=0)
        for b in range(3)
    ]
    kernel = jnp.concatenate([jnp.transpose(block.astype(F32)) for block in blocks], axis=0)
    product[:, width:-width] = jnp.dot(
        kernel.astype(BF16), stacked[...], preferred_element_type=F32
    )
    edge = jnp.zeros((product.shape[0], width), F32)
    product[:, :width] = edge
    product[:, -width:] = edge
    repeats, each = own.shape[:2]
    ways = rows // (repeats * each)
    for slot in range(ways):
        kind = lax.rem(place[0] + slot, ways)
        for q in range(repeats):
            for e in range(each):
                row = (q * ways + kind) * each + e
                (own, ahead, far, behind)[slot][q, e] = row_total(product, cout, row, width)


def sum_kernel(own, far, ahead, behind, out):
    out[...] = (own[...] + far[...]) + (ahead[...] + behind[...])


def pair_sum_kernel(kept, came, out):
    out[...] = kept[...] + came[...]


def backward_kernel(place, low, mid, high, weights, kept, handed, stacked, product):
    rows, cout, width = mid.shape
    cin = weights.shape[-2]
    stack_taps((low[...], mid[...], high[...]), stacked)
    kernel = jnp.concatenate(
        [
            jnp.concatenate(
                [weights[2 - a, 2 - b, 2 - c] for a in range(3) for c in range(3)], axis=1
            )
            for b in range(3)
        ],
        axis=0,
    )
    product[:, width:-width] = jnp.dot(kernel, stacked[...], preferred_element_type=F32)
    edge = jnp.zeros((product.shape[0], width), F32)
    product[:, :width] = edge
    product[:, -width:] = edge
    chips, share = kept.shape[:2]
    core = lax.rem(place[0], 2)
    for part, at_core in ((kept, core), (handed, 1 - core)):
        for chip in range(chips):
            for e in range(share):
                part[chip, e] = row_total(product, cin, (chip * 2 + at_core) * share + e, width)


def kernel_grad_kernel(planes, grad, out, stacked, shifted_grad):
    rows = grad.shape[0]
    cin, width = planes.shape[-2:]
    cout = grad.shape[1]
    stack_taps([planes[:, a].reshape(rows, cin, width) for a in range(3)], stacked)
    for b in range(3):
        for h in range(rows):
            row = h - (b - 1)
            value = grad[row] if 0 <= row < rows else jnp.zeros((cout, width), BF16)
            shifted_grad[b * cout : (b + 1) * cout, h * width : (h + 1) * width] = value
    taps = lax.dot_general(
        stacked[...], shifted_grad[...], (((1,), (1,)), ((), ())), preferred_element_type=F32
    )
    half = taps.shape[0] // 2
    first = taps[:, : 2 * cout]
    second = jnp.concatenate([taps[:half, 2 * cout :], taps[half:, 2 * cout :]], axis=1)
    rest = out.shape[0] - first.shape[0] - half
    out[: 2 * half] = first
    out[2 * half : 3 * half] = second
    out[3 * half :] = jnp.zeros((rest, 2 * cout), F32)


def kernel_grad_finish(scale, near, far, out):
    taps = ((near[...] + far[...]) * scale).astype(BF16)
    cin, cout = out.shape[-2:]
    half = 9 * cin // 2
    for a in range(3):
        for c in range(3):
            at = (a * 3 + c) * cin
            for b in range(2):
                out[a, b, c] = taps[at : at + cin, b * cout : (b + 1) * cout]
            for lo in range(at, at + cin, cin // 2):
                side = lo // half
                row = 2 * half + lo - side * half
                out[a, 2, c, lo - at : lo - at + cin // 2] = taps[
                    row : row + cin // 2, side * cout : (side + 1) * cout
                ]


def call(kernel, out, scratch, flops, *args):
    moved = sum(math.prod(a.shape) * a.dtype.itemsize for a in args)
    specs = [pl.BlockSpec(memory_space=pltpu.SMEM if a.ndim == 1 else pltpu.VMEM) for a in args]
    return pl.pallas_call(
        kernel,
        out_shape=out,
        in_specs=specs,
        scratch_shapes=scratch,
        compiler_params=pltpu.CompilerParams(vmem_limit_bytes=VMEM_LIMIT),
        cost_estimate=pl.CostEstimate(flops=flops, bytes_accessed=moved, transcendentals=0),
    )(*args)


def halos(plane, axis):
    count = lax.axis_size(axis)
    forward = [(i, i + 1) for i in range(count - 1)]
    backward = [(i + 1, i) for i in range(count - 1)]
    return lax.ppermute(plane, axis, forward), lax.ppermute(plane, axis, backward)


def around(block, axis, step):
    count = lax.axis_size(axis)
    return lax.ppermute(block, axis, [(i, (i + step) % count) for i in range(count)])


def around_by_core(block):
    ring, cores = lax.axis_size("cin"), lax.axis_size("cout")
    pairs = [
        (z * cores + y, (z + (2 if y % 2 == 0 else -2)) % ring * cores + y)
        for z in range(ring)
        for y in range(cores)
    ]
    return lax.ppermute(block, ("cin", "cout"), pairs)


def exchange(blocks, axis, groups=None):
    return lax.all_to_all(blocks, axis, 0, 0, tiled=True, axis_index_groups=groups)


def body(activations, weights, out_grad):
    cin, cout = weights.shape[3:]
    width = activations.shape[-1]
    ring = lax.axis_size("cin")
    depth = lax.axis_size("sp")
    ways = 4
    repeats = ring // ways
    apart = [[ways * q + r for q in range(repeats)] for r in range(ways)]
    x_own = jnp.transpose(activations[:, 0], (1, 0, 2))
    g_own = jnp.transpose(out_grad[:, 0], (1, 0, 2))
    each = g_own.shape[0]

    x_low, x_high = halos(x_own, "sp")
    g_copies = jnp.broadcast_to(g_own[None], (ring,) + g_own.shape)
    g_copies, x_low, x_high = lax.optimization_barrier((g_copies, x_low, x_high))
    g_mid = exchange(g_copies, "cin").reshape((-1,) + g_own.shape[1:])
    x_all = lax.all_gather(jnp.stack([x_low, x_own, x_high]), "cout", axis=0)
    rows = x_all.shape[0] * x_all.shape[2]
    voxels = rows * width
    flops = 2 * 27 * cin * cout * voxels

    piece = jax.ShapeDtypeStruct((repeats, each, cout, width), F32)
    place = lax.axis_index("cin").astype(jnp.int32).reshape(1)
    own, ahead, far, behind = call(
        forward_kernel,
        (piece, piece, piece, piece),
        [
            pltpu.VMEM((9 * cin, voxels), BF16),
            pltpu.VMEM((3 * cout, voxels + 2 * width), F32),
        ],
        flops,
        place,
        x_all,
        weights,
    )
    g_mid, own = lax.optimization_barrier((g_mid, own))
    g_low, g_high = halos(g_mid, "sp")
    packed_rows = -(-27 * cin // 2 // 32) * 32
    local_grad = call(
        kernel_grad_kernel,
        jax.ShapeDtypeStruct((packed_rows, 2 * cout), F32),
        [pltpu.VMEM((9 * cin, voxels), BF16), pltpu.VMEM((3 * cout, voxels), BF16)],
        flops,
        x_all,
        g_mid,
    )
    local_grad, own = lax.optimization_barrier((local_grad, own))
    near_sum = call(
        sum_kernel,
        piece,
        [],
        4 * math.prod(piece.shape),
        own,
        around_by_core(far),
        around(ahead, "cin", 1),
        around(behind, "cin", -1),
    )
    near_grad = lax.ppermute(local_grad, "sp", [(i, i ^ 1) for i in range(depth)])
    near_sum, g_mid = lax.optimization_barrier((near_sum, g_mid))
    near_grad, g_mid = lax.optimization_barrier((near_grad, g_mid))
    out_parts = exchange(near_sum, "cin", apart)

    cores = 2
    chips = lax.axis_size("cout") // cores
    share = rows // (chips * cores)
    place = lax.axis_index("cout").astype(jnp.int32).reshape(1)
    chunks = jax.ShapeDtypeStruct((chips, share, cin, width), F32)
    chunk = jax.ShapeDtypeStruct((share, cin, width), F32)
    kept, handed = call(
        backward_kernel,
        (chunks, chunks),
        [
            pltpu.VMEM((9 * cout, voxels), BF16),
            pltpu.VMEM((3 * cin, voxels + 2 * width), F32),
        ],
        flops,
        place,
        g_low,
        g_mid,
        g_high,
        weights,
    )
    came = lax.ppermute(handed, "cout", [(i, i ^ 1) for i in range(chips * cores)])
    pair_dx = call(pair_sum_kernel, chunks, [], math.prod(chunks.shape), kept, came)
    pair_grad = local_grad + near_grad
    far_grad = lax.ppermute(pair_grad, "sp", [(i, depth - 1 - i) for i in range(depth)])
    pair_dx, out_parts = lax.optimization_barrier((pair_dx, out_parts))
    same_core = [[cores * y + core for y in range(chips)] for core in range(cores)]
    dx_parts = exchange(
        pair_dx.reshape((chips * share, cin, width)), "cout", same_core
    ).reshape(chunks.shape)

    scale = 1.0 / math.sqrt(depth * voxels)
    weight_grad = call(
        functools.partial(kernel_grad_finish, scale),
        jax.ShapeDtypeStruct(weights.shape, BF16),
        [],
        27 * cin * cout * 2,
        pair_grad,
        far_grad,
    )

    def placed_as(summed, like):
        return jnp.transpose(summed, (1, 0, 2)).astype(BF16).reshape(like.shape)

    out_total = jnp.sum(out_parts, axis=0)
    return placed_as(out_total, out_grad), placed_as(jnp.sum(dx_parts, axis=0), activations), weight_grad


def solution(mesh):
    placed = (
        P("cin", "sp", "cout", None),
        P(None, None, None, "cin", "cout"),
        P("cout", "sp", "cin", None),
    )
    return jax.shard_map(
        body,
        mesh=mesh,
        in_specs=placed,
        out_specs=(
            P("cout", "sp", "cin", None),
            P("cin", "sp", "cout", None),
            P(None, None, None, "cin", "cout"),
        ),
        check_vma=False,
    )
```

```python
import functools
import math

import jax
import jax.numpy as jnp
from jax import lax
from jax.experimental import pallas as pl
from jax.experimental.pallas import tpu as pltpu
from jax.sharding import PartitionSpec as P

F32 = jnp.float32
BF16 = jnp.bfloat16
VMEM_LIMIT = 40 * 1024 * 1024


def shifted(plane, step):
    if step == 0:
        return plane
    width = plane.shape[-1]
    moved = pltpu.roll(plane.astype(F32), (-step) % width, plane.ndim - 1)
    lane = lax.broadcasted_iota(jnp.int32, plane.shape, plane.ndim - 1)
    edge = width - 1 if step > 0 else 0
    return jnp.where(lane == edge, 0.0, moved).astype(plane.dtype)


def stack_taps(planes, stacked):
    rows, channels, width = planes[0].shape
    for a, plane in enumerate(planes):
        value = plane
        for c in range(3):
            moved = shifted(value, c - 1)
            at = (a * 3 + c) * channels
            for h in range(rows):
                stacked[at : at + channels, h * width : (h + 1) * width] = moved[h]


def row_total(product, channels, row, width):
    total = None
    for b in range(3):
        at = pl.multiple_of((row + b) * width, width)
        part = product[b * channels : (b + 1) * channels, pl.ds(at, width)]
        total = part if total is None else total + part
    return total


def forward_kernel(place, planes, weights, own, ahead, far, behind, stacked, product):
    cin, width = planes.shape[-2:]
    rows = planes.shape[0] * planes.shape[2]
    cout = weights.shape[-1]
    stack_taps([planes[:, a].reshape(rows, cin, width) for a in range(3)], stacked)
    blocks = [
        jnp.concatenate([weights[a, b, c] for a in range(3) for c in range(3)], axis=0)
        for b in range(3)
    ]
    kernel = jnp.concatenate([jnp.transpose(block.astype(F32)) for block in blocks], axis=0)
    product[:, width:-width] = jnp.dot(
        kernel.astype(BF16), stacked[...], preferred_element_type=F32
    )
    edge = jnp.zeros((product.shape[0], width), F32)
    product[:, :width] = edge
    product[:, -width:] = edge
    repeats, each = own.shape[:2]
    ways = rows // (repeats * each)
    for slot in range(ways):
        kind = lax.rem(place[0] + slot, ways)
        for q in range(repeats):
            for e in range(each):
                row = (q * ways + kind) * each + e
                (own, ahead, far, behind)[slot][q, e] = row_total(product, cout, row, width)


def sum_kernel(own, far, ahead, behind, out):
    out[...] = (own[...] + far[...]) + (ahead[...] + behind[...])


def split_sum_kernel(kept, came, mine, far, ahead, behind):
    for slot, part in enumerate((mine, ahead, far, behind)):
        part[...] = kept[slot] + came[slot]


def backward_kernel(place, low, mid, high, weights, kept, handed, stacked, product):
    rows, cout, width = mid.shape
    cin = weights.shape[-2]
    stack_taps((low[...], mid[...], high[...]), stacked)
    kernel = jnp.concatenate(
        [
            jnp.concatenate(
                [weights[2 - a, 2 - b, 2 - c] for a in range(3) for c in range(3)], axis=1
            )
            for b in range(3)
        ],
        axis=0,
    )
    product[:, width:-width] = jnp.dot(kernel, stacked[...], preferred_element_type=F32)
    edge = jnp.zeros((product.shape[0], width), F32)
    product[:, :width] = edge
    product[:, -width:] = edge
    chips, share = kept.shape[:2]
    chip, core = lax.div(place[0], 2), lax.rem(place[0], 2)
    for part, at_core in ((kept, core), (handed, 1 - core)):
        for slot in range(chips):
            at_chip = lax.rem(chip + slot, chips)
            for e in range(share):
                part[slot, e] = row_total(product, cin, (at_chip * 2 + at_core) * share + e, width)


def kernel_grad_kernel(planes, grad, out, stacked, shifted_grad):
    rows = grad.shape[0]
    cin, width = planes.shape[-2:]
    cout = grad.shape[1]
    stack_taps([planes[:, a].reshape(rows, cin, width) for a in range(3)], stacked)
    for b in range(3):
        for h in range(rows):
            row = h - (b - 1)
            value = grad[row] if 0 <= row < rows else jnp.zeros((cout, width), BF16)
            shifted_grad[b * cout : (b + 1) * cout, h * width : (h + 1) * width] = value
    taps = lax.dot_general(
        stacked[...], shifted_grad[...], (((1,), (1,)), ((), ())), preferred_element_type=F32
    )
    half = taps.shape[0] // 2
    first = taps[:, : 2 * cout]
    second = jnp.concatenate([taps[:half, 2 * cout :], taps[half:, 2 * cout :]], axis=1)
    rest = out.shape[0] - first.shape[0] - half
    out[: 2 * half] = first
    out[2 * half : 3 * half] = second
    out[3 * half :] = jnp.zeros((rest, 2 * cout), F32)


def kernel_grad_finish(scale, near, far, out):
    taps = ((near[...] + far[...]) * scale).astype(BF16)
    cin, cout = out.shape[-2:]
    half = 9 * cin // 2
    for a in range(3):
        for c in range(3):
            at = (a * 3 + c) * cin
            for b in range(2):
                out[a, b, c] = taps[at : at + cin, b * cout : (b + 1) * cout]
            for lo in range(at, at + cin, cin // 2):
                side = lo // half
                row = 2 * half + lo - side * half
                out[a, 2, c, lo - at : lo - at + cin // 2] = taps[
                    row : row + cin // 2, side * cout : (side + 1) * cout
                ]


def call(kernel, out, scratch, flops, *args):
    moved = sum(math.prod(a.shape) * a.dtype.itemsize for a in args)
    specs = [pl.BlockSpec(memory_space=pltpu.SMEM if a.ndim == 1 else pltpu.VMEM) for a in args]
    return pl.pallas_call(
        kernel,
        out_shape=out,
        in_specs=specs,
        scratch_shapes=scratch,
        compiler_params=pltpu.CompilerParams(vmem_limit_bytes=VMEM_LIMIT),
        cost_estimate=pl.CostEstimate(flops=flops, bytes_accessed=moved, transcendentals=0),
    )(*args)


def halos(plane, axis):
    count = lax.axis_size(axis)
    forward = [(i, i + 1) for i in range(count - 1)]
    backward = [(i + 1, i) for i in range(count - 1)]
    return lax.ppermute(plane, axis, forward), lax.ppermute(plane, axis, backward)


def around(block, axis, step):
    count = lax.axis_size(axis)
    return lax.ppermute(block, axis, [(i, (i + step) % count) for i in range(count)])


def around_by_core(block):
    ring, cores = lax.axis_size("cin"), lax.axis_size("cout")
    pairs = [
        (z * cores + y, (z + (2 if y % 2 == 0 else -2)) % ring * cores + y)
        for z in range(ring)
        for y in range(cores)
    ]
    return lax.ppermute(block, ("cin", "cout"), pairs)


def exchange(blocks, axis, groups=None):
    return lax.all_to_all(blocks, axis, 0, 0, tiled=True, axis_index_groups=groups)


def body(activations, weights, out_grad):
    cin, cout = weights.shape[3:]
    width = activations.shape[-1]
    ring = lax.axis_size("cin")
    depth = lax.axis_size("sp")
    ways = 4
    repeats = ring // ways
    apart = [[ways * q + r for q in range(repeats)] for r in range(ways)]
    x_own = jnp.transpose(activations[:, 0], (1, 0, 2))
    g_own = jnp.transpose(out_grad[:, 0], (1, 0, 2))
    each = g_own.shape[0]

    x_low, x_high = halos(x_own, "sp")
    g_copies = jnp.broadcast_to(g_own[None], (ring,) + g_own.shape)
    g_mid = exchange(g_copies, "cin").reshape((-1,) + g_own.shape[1:])
    x_all = lax.all_gather(jnp.stack([x_low, x_own, x_high]), "cout", axis=0)
    rows = x_all.shape[0] * x_all.shape[2]
    voxels = rows * width
    flops = 2 * 27 * cin * cout * voxels

    piece = jax.ShapeDtypeStruct((repeats, each, cout, width), F32)
    place = lax.axis_index("cin").astype(jnp.int32).reshape(1)
    own, ahead, far, behind = call(
        forward_kernel,
        (piece, piece, piece, piece),
        [
            pltpu.VMEM((9 * cin, voxels), BF16),
            pltpu.VMEM((3 * cout, voxels + 2 * width), F32),
        ],
        40 * flops,
        place,
        x_all,
        weights,
    )
    g_mid, own = lax.optimization_barrier((g_mid, own))
    g_low, g_high = halos(g_mid, "sp")
    packed_rows = -(-27 * cin // 2 // 32) * 32
    local_grad = call(
        kernel_grad_kernel,
        jax.ShapeDtypeStruct((packed_rows, 2 * cout), F32),
        [pltpu.VMEM((9 * cin, voxels), BF16), pltpu.VMEM((3 * cout, voxels), BF16)],
        flops,
        x_all,
        g_mid,
    )
    local_grad, own = lax.optimization_barrier((local_grad, own))
    near_sum = call(
        sum_kernel,
        piece,
        [],
        40 * flops,
        own,
        around_by_core(far),
        around(ahead, "cin", 1),
        around(behind, "cin", -1),
    )
    near_grad = lax.ppermute(local_grad, "sp", [(i, i ^ 1) for i in range(depth)])
    near_sum, g_mid = lax.optimization_barrier((near_sum, g_mid))
    out_parts = exchange(near_sum, "cin", apart)

    cores = 2
    chips = lax.axis_size("cout") // cores
    share = rows // (chips * cores)
    place = lax.axis_index("cout").astype(jnp.int32).reshape(1)
    chunks = jax.ShapeDtypeStruct((chips, share, cin, width), F32)
    chunk = jax.ShapeDtypeStruct((share, cin, width), F32)
    kept, handed = call(
        backward_kernel,
        (chunks, chunks),
        [
            pltpu.VMEM((9 * cout, voxels), BF16),
            pltpu.VMEM((3 * cin, voxels + 2 * width), F32),
        ],
        40 * flops,
        place,
        g_low,
        g_mid,
        g_high,
        weights,
    )
    came = lax.ppermute(handed, "cout", [(i, i ^ 1) for i in range(chips * cores)])
    pair_grad = local_grad + near_grad
    far_grad = lax.ppermute(pair_grad, "sp", [(i, depth - 1 - i) for i in range(depth)])
    mine, far, ahead, behind = call(
        split_sum_kernel, (chunk, chunk, chunk, chunk), [], math.prod(chunks.shape), kept, came
    )

    def chip_step(block, step):
        count = chips * cores
        return lax.ppermute(block, "cout", [(i, (i + cores * step) % count) for i in range(count)])

    dx_total = call(
        sum_kernel,
        chunk,
        [],
        4 * math.prod(chunk.shape),
        mine,
        chip_step(far, 2),
        chip_step(ahead, 1),
        chip_step(behind, -1),
    )

    scale = 1.0 / math.sqrt(depth * voxels)
    weight_grad = call(
        functools.partial(kernel_grad_finish, scale),
        jax.ShapeDtypeStruct(weights.shape, BF16),
        [],
        27 * cin * cout * 2,
        pair_grad,
        far_grad,
    )

    def placed_as(summed, like):
        return jnp.transpose(summed, (1, 0, 2)).astype(BF16).reshape(like.shape)

    out_total = jnp.sum(out_parts, axis=0)
    return placed_as(out_total, out_grad), placed_as(dx_total, activations), weight_grad


def solution(mesh):
    placed = (
        P("cin", "sp", "cout", None),
        P(None, None, None, "cin", "cout"),
        P("cout", "sp", "cin", None),
    )
    return jax.shard_map(
        body,
        mesh=mesh,
        in_specs=placed,
        out_specs=(
            P("cout", "sp", "cin", None),
            P("cin", "sp", "cout", None),
            P(None, None, None, "cin", "cout"),
        ),
        check_vma=False,
    )
```

```python
import functools
import math

import jax
import jax.numpy as jnp
from jax import lax
from jax.experimental import pallas as pl
from jax.experimental.pallas import tpu as pltpu
from jax.sharding import PartitionSpec as P

F32 = jnp.float32
BF16 = jnp.bfloat16
VMEM_LIMIT = 16 * 1024 * 1024


def shifted(plane, step):
    if step == 0:
        return plane
    width = plane.shape[-1]
    moved = pltpu.roll(plane, (-step) % width, plane.ndim - 1)
    lane = lax.broadcasted_iota(jnp.int32, plane.shape, plane.ndim - 1)
    edge = width - 1 if step > 0 else 0
    return jnp.where(lane == edge, jnp.zeros_like(moved), moved)


def stack_taps(planes, stacked):
    rows, channels, width = planes[0].shape
    for a, plane in enumerate(planes):
        value = plane
        for c in range(3):
            moved = shifted(value, c - 1)
            at = (a * 3 + c) * channels
            for h in range(rows):
                stacked[at : at + channels, h * width : (h + 1) * width] = moved[h]


def row_total(product, channels, row, width):
    total = None
    for b in range(3):
        at = pl.multiple_of((row + b) * width, width)
        part = product[b * channels : (b + 1) * channels, pl.ds(at, width)]
        total = part if total is None else total + part
    return total


def forward_kernel(place, planes, weights, own, ahead, far, behind, stacked, product):
    cin, width = planes.shape[-2:]
    rows = planes.shape[0] * planes.shape[2]
    cout = weights.shape[-1]
    stack_taps([planes[:, a].reshape(rows, cin, width) for a in range(3)], stacked)
    blocks = [
        jnp.concatenate([weights[a, b, c] for a in range(3) for c in range(3)], axis=0)
        for b in range(3)
    ]
    kernel = jnp.concatenate([jnp.transpose(block.astype(F32)) for block in blocks], axis=0)
    product[:, width:-width] = jnp.dot(
        kernel.astype(BF16), stacked[...], preferred_element_type=F32
    )
    edge = jnp.zeros((product.shape[0], width), F32)
    product[:, :width] = edge
    product[:, -width:] = edge
    repeats, each = own.shape[:2]
    ways = rows // (repeats * each)
    for slot in range(ways):
        kind = lax.rem(place[0] + slot, ways)
        for q in range(repeats):
            for e in range(each):
                row = (q * ways + kind) * each + e
                (own, ahead, far, behind)[slot][q, e] = row_total(product, cout, row, width)


def sum_kernel(first, second, third, fourth, out):
    out[...] = (first[...] + second[...]) + (third[...] + fourth[...])


def split_sum_kernel(kept, came, mine, far, ahead, behind):
    for slot, part in enumerate((mine, ahead, far, behind)):
        part[...] = kept[slot] + came[slot]


def backward_kernel(place, low, mid, high, weights, kept, handed, stacked, product):
    rows, cout, width = mid.shape
    cin = weights.shape[-2]
    stack_taps((low[...], mid[...], high[...]), stacked)
    kernel = jnp.concatenate(
        [
            jnp.concatenate(
                [weights[2 - a, 2 - b, 2 - c] for a in range(3) for c in range(3)], axis=1
            )
            for b in range(3)
        ],
        axis=0,
    )
    product[:, width:-width] = jnp.dot(kernel, stacked[...], preferred_element_type=F32)
    edge = jnp.zeros((product.shape[0], width), F32)
    product[:, :width] = edge
    product[:, -width:] = edge
    chips, share = kept.shape[:2]
    chip, core = lax.div(place[0], 2), lax.rem(place[0], 2)
    for part, at_core in ((kept, core), (handed, 1 - core)):
        for slot in range(chips):
            at_chip = lax.rem(chip + slot, chips)
            for e in range(share):
                part[slot, e] = row_total(product, cin, (at_chip * 2 + at_core) * share + e, width)


def kernel_grad_kernel(planes, grad, out, stacked, shifted_grad):
    rows = grad.shape[0]
    cin, width = planes.shape[-2:]
    cout = grad.shape[1]
    stack_taps([planes[:, a].reshape(rows, cin, width) for a in range(3)], stacked)
    for b in range(3):
        for h in range(rows):
            row = h - (b - 1)
            value = grad[row] if 0 <= row < rows else jnp.zeros((cout, width), BF16)
            shifted_grad[b * cout : (b + 1) * cout, h * width : (h + 1) * width] = value
    taps = lax.dot_general(
        stacked[...], shifted_grad[...], (((1,), (1,)), ((), ())), preferred_element_type=F32
    )
    half = taps.shape[0] // 2
    first = taps[:, : 2 * cout]
    second = jnp.concatenate([taps[:half, 2 * cout :], taps[half:, 2 * cout :]], axis=1)
    rest = out.shape[0] - first.shape[0] - half
    out[: 2 * half] = first
    out[2 * half : 3 * half] = second
    out[3 * half :] = jnp.zeros((rest, 2 * cout), F32)


def kernel_grad_finish(scale, near, far, out):
    taps = ((near[...] + far[...]) * scale).astype(BF16)
    cin, cout = out.shape[-2:]
    half = 9 * cin // 2
    for a in range(3):
        for c in range(3):
            at = (a * 3 + c) * cin
            for b in range(2):
                out[a, b, c] = taps[at : at + cin, b * cout : (b + 1) * cout]
            for lo in range(at, at + cin, cin // 2):
                side = lo // half
                row = 2 * half + lo - side * half
                out[a, 2, c, lo - at : lo - at + cin // 2] = taps[
                    row : row + cin // 2, side * cout : (side + 1) * cout
                ]


def call(kernel, out, scratch, flops, *args):
    moved = sum(math.prod(a.shape) * a.dtype.itemsize for a in args)
    specs = [pl.BlockSpec(memory_space=pltpu.SMEM if a.ndim == 1 else pltpu.VMEM) for a in args]
    return pl.pallas_call(
        kernel,
        out_shape=out,
        in_specs=specs,
        scratch_shapes=scratch,
        compiler_params=pltpu.CompilerParams(vmem_limit_bytes=VMEM_LIMIT),
        cost_estimate=pl.CostEstimate(flops=flops, bytes_accessed=moved, transcendentals=0),
    )(*args)


def halos(plane, axis):
    count = lax.axis_size(axis)
    forward = [(i, i + 1) for i in range(count - 1)]
    backward = [(i + 1, i) for i in range(count - 1)]
    return lax.ppermute(plane, axis, forward), lax.ppermute(plane, axis, backward)


def around(block, axis, step):
    count = lax.axis_size(axis)
    return lax.ppermute(block, axis, [(i, (i + step) % count) for i in range(count)])


def around_by_core(block):
    ring, cores = lax.axis_size("cin"), lax.axis_size("cout")
    pairs = [
        (z * cores + y, (z + (2 if y % 2 == 0 else -2)) % ring * cores + y)
        for z in range(ring)
        for y in range(cores)
    ]
    return lax.ppermute(block, ("cin", "cout"), pairs)


def exchange(blocks, axis, groups=None):
    return lax.all_to_all(blocks, axis, 0, 0, tiled=True, axis_index_groups=groups)


def body(activations, weights, out_grad):
    cin, cout = weights.shape[3:]
    width = activations.shape[-1]
    ring = lax.axis_size("cin")
    depth = lax.axis_size("sp")
    ways = 4
    repeats = ring // ways
    apart = [[ways * q + r for q in range(repeats)] for r in range(ways)]
    x_own = jnp.transpose(activations[:, 0], (1, 0, 2))
    g_own = jnp.transpose(out_grad[:, 0], (1, 0, 2))
    each = g_own.shape[0]

    x_low, x_high = halos(x_own, "sp")
    g_copies = jnp.broadcast_to(g_own[None], (ring,) + g_own.shape)
    g_mid = exchange(g_copies, "cin").reshape((-1,) + g_own.shape[1:])
    x_all = lax.all_gather(jnp.stack([x_low, x_own, x_high]), "cout", axis=0)
    rows = x_all.shape[0] * x_all.shape[2]
    voxels = rows * width
    flops = 2 * 27 * cin * cout * voxels

    piece = jax.ShapeDtypeStruct((repeats, each, cout, width), F32)
    place = lax.axis_index("cin").astype(jnp.int32).reshape(1)
    own, ahead, far, behind = call(
        forward_kernel,
        (piece, piece, piece, piece),
        [
            pltpu.VMEM((9 * cin, voxels), BF16),
            pltpu.VMEM((3 * cout, voxels + 2 * width), F32),
        ],
        40 * flops,
        place,
        x_all,
        weights,
    )
    g_mid, own = lax.optimization_barrier((g_mid, own))
    g_low, g_high = halos(g_mid, "sp")
    packed_rows = -(-27 * cin // 2 // 32) * 32
    local_grad = call(
        kernel_grad_kernel,
        jax.ShapeDtypeStruct((packed_rows, 2 * cout), F32),
        [pltpu.VMEM((9 * cin, voxels), BF16), pltpu.VMEM((3 * cout, voxels), BF16)],
        flops,
        x_all,
        g_mid,
    )
    local_grad, own = lax.optimization_barrier((local_grad, own))
    near_sum = call(
        sum_kernel,
        piece,
        [],
        40 * flops,
        own,
        around(ahead, "cin", 1),
        around(behind, "cin", -1),
        around_by_core(far),
    )
    near_grad = lax.ppermute(local_grad, "sp", [(i, i ^ 1) for i in range(depth)])
    near_sum, g_mid = lax.optimization_barrier((near_sum, g_mid))
    out_parts = exchange(near_sum, "cin", apart)

    cores = 2
    chips = lax.axis_size("cout") // cores
    share = rows // (chips * cores)
    place = lax.axis_index("cout").astype(jnp.int32).reshape(1)
    chunks = jax.ShapeDtypeStruct((chips, share, cin, width), F32)
    chunk = jax.ShapeDtypeStruct((share, cin, width), F32)
    kept, handed = call(
        backward_kernel,
        (chunks, chunks),
        [
            pltpu.VMEM((9 * cout, voxels), BF16),
            pltpu.VMEM((3 * cin, voxels + 2 * width), F32),
        ],
        40 * flops,
        place,
        g_low,
        g_mid,
        g_high,
        weights,
    )
    came = lax.ppermute(handed, "cout", [(i, i ^ 1) for i in range(chips * cores)])
    pair_grad = local_grad + near_grad
    far_grad = lax.ppermute(pair_grad, "sp", [(i, depth - 1 - i) for i in range(depth)])
    mine, far, ahead, behind = call(
        split_sum_kernel, (chunk, chunk, chunk, chunk), [], math.prod(chunks.shape), kept, came
    )

    def chip_step(block, step):
        count = chips * cores
        return lax.ppermute(block, "cout", [(i, (i + cores * step) % count) for i in range(count)])

    dx_total = call(
        sum_kernel,
        chunk,
        [],
        4 * math.prod(chunk.shape),
        mine,
        chip_step(far, 2),
        chip_step(ahead, 1),
        chip_step(behind, -1),
    )

    scale = 1.0 / math.sqrt(depth * voxels)
    weight_grad = call(
        functools.partial(kernel_grad_finish, scale),
        jax.ShapeDtypeStruct(weights.shape, BF16),
        [],
        27 * cin * cout * 2,
        pair_grad,
        far_grad,
    )

    def placed_as(summed, like):
        return jnp.transpose(summed, (1, 0, 2)).astype(BF16).reshape(like.shape)

    out_total = jnp.sum(out_parts, axis=0)
    return placed_as(out_total, out_grad), placed_as(dx_total, activations), weight_grad


def solution(mesh):
    placed = (
        P("cin", "sp", "cout", None),
        P(None, None, None, "cin", "cout"),
        P("cout", "sp", "cin", None),
    )
    return jax.shard_map(
        body,
        mesh=mesh,
        in_specs=placed,
        out_specs=(
            P("cout", "sp", "cin", None),
            P("cin", "sp", "cout", None),
            P(None, None, None, "cin", "cout"),
        ),
        check_vma=False,
    )
```
